32 devices in a mesh: row: 4 (over y, x), col: 8 (over z, core).
Axes of the slice: x: 2, y: 2, z: 4, core: 2. Of those that a mesh axis runs over, the one named last changes fastest.
Arguments:
- trail_adjoint: float32 [32, 512, 16, 1024], P(None, 'row', None, 'col'), may hold values from -6 to 6
- panel: float32 [32, 512, 128], P(None, 'row'), may hold values from -0.046875 to 0.046875
- panel_adjoint: float32 [32, 512, 128], P(None, 'row'), may hold values from -6 to 6
- diag_block: float32 [128, 128], replicated, as said below
Outputs:
- input_adjoint: float32 [32, 512, 128], P(None, 'row')
- block_adjoint: float32 [128, 128], replicated
The draws below stay inside these ranges and needn't reach their ends.
Inputs may be any that keep to these rules, and one draw needn't show every extreme that they name: diag_block is lower triangular with diagonal entries between 1.5 and 3 and zeros above the diagonal.
All inputs are finite; a program needn't handle non-finite values.
Results may differ from the reference program's by a relative error of at most 0.000082.
Values sent between devices are 32-bit elements; how exact they have to be, the bound alone decides.
No kernel may reach another device: no remote copies, remote signals or barrier semaphores. Data moves between devices by JAX's collectives and lax.ppermute only.
A program may use at most 128 MiB of HBM per device.

```python
import jax
import jax.numpy as jnp
from jax import lax

M = 16384
BLK = 128
RB = 32
CB = 16
N_ROW = 4
N_COL = 8


def draw_diag_block(key, part):
    first, second = jax.random.split(jax.random.fold_in(key, 11))
    lower_part = jax.random.normal(first, (BLK, BLK), jnp.float32) * (1.0 / BLK) ** 0.5
    diagonal = jax.random.uniform(second, (BLK,), jnp.float32, 1.5, 3.0)
    return jnp.tril(lower_part, -1) + jnp.diag(diagonal)


def block_levels(key, shape, cuts, low, top_value):
    loudness, own = 1.0, jax.random.fold_in(key, 6)
    for axis_at, shards_of in cuts:
        draws = jnp.exp(jax.random.uniform(jax.random.fold_in(own, axis_at), (shards_of,), jnp.float32, low / len(cuts), top_value / len(cuts)))
        loudness = loudness * jnp.repeat(draws, shape[axis_at] // shards_of).reshape([-1 if axis == axis_at else 1 for axis in range(len(shape))])
    return loudness


def centred(own_key, dims, width, bound, shards=(), held_as=jnp.bfloat16):
    drawn = jax.random.normal(own_key, dims, jnp.float32) * width
    if len(shards) > 0:
        drawn = block_levels(own_key, dims, shards, -0.22, 0.18) * drawn
    return jnp.clip(drawn, min=-bound, max=bound).astype(held_as)


def setup_inputs(seed: int = 0) -> dict:
    keys = jax.random.split(jax.random.key(seed), 5)
    trail_adjoint = centred(keys[0], (RB, N_ROW * BLK, CB, N_COL * BLK), 1.0, 6.0, ((1, 4), (3, 8)), jnp.float32)
    panel = centred(keys[1], (RB, N_ROW * BLK, BLK), M ** -0.5, 0.046875, ((1, 4),), jnp.float32)
    panel_adjoint = centred(keys[2], (RB, N_ROW * BLK, BLK), 1.0, 6.0, ((1, 4),), jnp.float32)
    diag_block = draw_diag_block(jax.random.fold_in(keys[4], 71), 0)
    return {"trail_adjoint": trail_adjoint, "panel": panel, "panel_adjoint": panel_adjoint, "diag_block": diag_block}


def reference(trail_adjoint, panel, panel_adjoint, diag_block):
    whole = trail_adjoint.reshape(M, M)
    factor = panel.reshape(M, BLK)
    given = panel_adjoint.reshape(M, BLK)
    direct = jnp.dot(whole.astype(jnp.float32), factor.astype(jnp.float32), precision=lax.Precision.HIGHEST, preferred_element_type=jnp.float32)
    flipped = jnp.dot(whole.T.astype(jnp.float32), factor.astype(jnp.float32), precision=lax.Precision.HIGHEST, preferred_element_type=jnp.float32)
    total = given - (direct + flipped)
    solved = lax.linalg.triangular_solve(diag_block, total, left_side=False, lower=True)
    gram = -jnp.dot(solved.T.astype(jnp.float32), factor.astype(jnp.float32), precision=lax.Precision.HIGHEST, preferred_element_type=jnp.float32)
    return (solved.reshape(RB, N_ROW * BLK, BLK), jnp.tril(gram))
```

```python
import functools
import math

import jax
import jax.numpy as jnp
from jax import lax
from jax.experimental import pallas as pl
from jax.experimental.pallas import tpu as pltpu
from jax.sharding import PartitionSpec as P

F32 = jnp.float32
BF16 = jnp.bfloat16
HIGHEST = lax.Precision.HIGHEST
AXES = ("row", "col")
KEEP_BYTES = 24 * 2**20
FLIP_VMEM = 20 * 2**20
DIRECT_VMEM = 12 * 2**20
CHUNK_VMEM = 24 * 2**20
SMALL_VMEM = 8 * 2**20


def split(x):
    high = x.astype(BF16)
    return high, (x - high.astype(F32)).astype(BF16)


def dot(a, b):
    return jnp.dot(a, b, preferred_element_type=F32)


def full_dot(a, b):
    return jnp.dot(a, b, preferred_element_type=F32, precision=HIGHEST)


def send(x, target, n_row, n_col):
    pairs = []
    for r in range(n_row):
        for c in range(n_col):
            to_r, to_c = target(r, c)
            pairs.append((r * n_col + c, to_r * n_col + to_c))
    return lax.ppermute(x, AXES, pairs)


def choose(grouped, which):
    blocks, _, width, _ = grouped.shape

    def body(which_ref, source, target):
        target[...] = source[...]

    return pl.pallas_call(
        body,
        grid_spec=pltpu.PrefetchScalarGridSpec(
            num_scalar_prefetch=1,
            grid=(1,),
            in_specs=[pl.BlockSpec((blocks, None, width, width), lambda i, which: (0, which[0], 0, 0))],
            out_specs=pl.BlockSpec((blocks, width, width), lambda i, which: (0, 0, 0)),
        ),
        out_shape=jax.ShapeDtypeStruct((blocks, width, width), F32),
        compiler_params=pltpu.CompilerParams(vmem_limit_bytes=SMALL_VMEM),
        name="choose",
    )(which, grouped)


def flip_body(plan, n_parts, me_ref, ids_ref, s_ref, l_ref, d_ref, *refs):
    outs, (inv_ref, high_ref, low_ref, acc, turned, buf, sems) = refs[:n_parts], refs[n_parts:]
    step, n_steps, slot = pl.program_id(0), plan.n_chunks, pl.program_id(0) % 2
    n_blocks, rows, width = plan.n_blocks, plan.chunk_rows, plan.width

    def fetch(i, slot):
        qb, h, qs = plan.chunk_at(ids_ref[plan.flip_place(i)])
        target = buf.at[slot]
        if plan.pitch > n_blocks:
            target = target.at[:, :, pl.ds(0, n_blocks), :]
        return pltpu.make_async_copy(s_ref.at[qb, :, h, qs], target, sems.at[slot])

    @pl.when(step == 0)
    def _():
        fetch(0, 0).start()
        acc[...] = jnp.zeros_like(acc)
        inv_ref[...] = inverse_start(d_ref[...])

    @pl.when(step + 1 < n_steps)
    def _():
        fetch(step + 1, 1 - slot).start()

    inv = inv_ref[...]
    for level in range(plan.levels_per_step):
        inv = inverse_level(d_ref[...], inv, step * plan.levels_per_step + level)
    inv_ref[...] = inv

    l_high, l_low = split(l_ref[...].reshape(rows, width))
    left = jnp.concatenate([l_high, l_low], 1).T
    fetch(step, slot).wait()
    flat = buf.at[slot].reshape(rows * plan.pitch, width)
    kept = pl.ds(pl.multiple_of(jnp.maximum(step - plan.skip, 0) * rows, rows), rows)
    for first in range(0, n_blocks, plan.group):
        x = jnp.concatenate(
            [flat[pl.ds(b, rows, stride=plan.pitch), :] for b in range(first, first + plan.group)], 1
        )
        high, low = split(x)
        here = pl.ds(first * width, plan.group * width)
        high_ref[kept, here] = high
        low_ref[kept, here] = low
        both = dot(left, high)
        acc[:, here] += both[:width] + both[width:] + dot(left[:width], low)

    @pl.when(step == n_steps - 1)
    def _():
        for b in range(n_blocks):
            here = pl.ds(b * width, width)
            turned[here, :] = acc[:, here].T
        size = outs[0].shape[0]
        for k, out in enumerate(outs):
            start = pl.multiple_of((me_ref[0] ^ k) * size, size)
            out[...] = turned[pl.ds(start, size), :]


def flip_parts(plan, trail, panel, diag_block, ids, me, n_row):
    width, n_blocks = plan.width, plan.n_blocks
    size = n_blocks * width // n_row
    kept = plan.keep * plan.chunk_rows
    qb, n_sub, ratio, qs, rows = plan.view
    if plan.pitch > n_blocks:
        source = trail.reshape(*plan.view, n_blocks, width)
        buffer = pltpu.VMEM((2, n_sub, rows, plan.pitch, width), F32)
    else:
        source = trail.reshape(*plan.view[:4], rows * n_blocks, width)
        buffer = pltpu.VMEM((2, n_sub, rows * n_blocks, width), F32)

    def l_index(i, me, ids):
        b, h, s = plan.chunk_at(ids[plan.flip_place(i)])
        return (b, 0, h, s, 0, 0)

    square = pl.BlockSpec((width, width), lambda i, me, ids: (0, 0))
    whole = pl.BlockSpec(memory_space=pltpu.VMEM)
    resident = pltpu.VMEM((kept, n_blocks * width), BF16)
    n = plan.n_chunks * plan.chunk_rows
    out = pl.pallas_call(
        functools.partial(flip_body, plan, n_row),
        grid_spec=pltpu.PrefetchScalarGridSpec(
            num_scalar_prefetch=2,
            grid=(plan.n_chunks,),
            in_specs=[
                pl.BlockSpec(memory_space=pl.ANY),
                pl.BlockSpec((None, n_sub, None, None, rows, width), l_index),
                square,
            ],
            out_specs=[pl.BlockSpec((size, width), lambda i, me, ids: (0, 0))] * n_row + [square, whole, whole],
            scratch_shapes=[
                pltpu.VMEM((width, n_blocks * width), F32),
                pltpu.VMEM((n_blocks * width, width), F32),
                buffer,
                pltpu.SemaphoreType.DMA((2,)),
            ],
        ),
        out_shape=[jax.ShapeDtypeStruct((size, width), F32)] * n_row
        + [jax.ShapeDtypeStruct((width, width), F32), resident, resident],
        compiler_params=pltpu.CompilerParams(vmem_limit_bytes=FLIP_VMEM),
        cost_estimate=pl.CostEstimate(
            flops=6 * n * n_blocks * width * width, bytes_accessed=4 * n * n_blocks * width, transcendentals=0
        ),
        name="flip",
    )(me, ids, source, panel.reshape(*plan.view, width), diag_block)
    return out[:n_row], out[n_row], out[n_row + 1], out[n_row + 2]


def inverse_start(d):
    i = lax.broadcasted_iota(jnp.int32, d.shape, 0)
    j = lax.broadcasted_iota(jnp.int32, d.shape, 1)
    return jnp.where(i == j, 1.0 / d, 0.0)


def inverse_level(d, inv, level):
    i = lax.broadcasted_iota(jnp.int32, d.shape, 0)
    j = lax.broadcasted_iota(jnp.int32, d.shape, 1)
    same = (i >> (level + 1)) == (j >> (level + 1))
    below = (i >> level) > (j >> level)
    part = jnp.where(jnp.logical_and(same, below), d, 0.0)
    return inv - full_dot(inv, full_dot(part, inv))


def direct_body(n_blocks, group, half, ids_ref, s_ref, p_ref, away_ref, keep_ref, right):
    step = pl.program_id(0)
    width = p_ref.shape[1]

    @pl.when(step == 0)
    def _():
        for g in range(n_blocks // group):
            high, low = split(p_ref[pl.ds(g * group * width, group * width), :])
            right[g, :, :width] = high
            right[g, :, width:] = low

    n_sub, sub_rows, _ = s_ref.shape
    rows = sub_rows // n_blocks

    def column(b):
        return jnp.concatenate([s_ref[i, pl.ds(b, rows, stride=n_blocks), :] for i in range(n_sub)], 0)

    both, rest = None, None
    for g in range(n_blocks // group):
        x = jnp.concatenate([column(g * group + b) for b in range(group)], 1)
        high, low = split(x)
        new_both = dot(high, right[g])
        new_rest = dot(low, right[g, :, :width])
        both = new_both if both is None else both + new_both
        rest = new_rest if rest is None else rest + new_rest
    result = both[:, :width] + both[:, width:] + rest

    @pl.when(step < half)
    def _():
        away_ref[...] = result

    @pl.when(step >= half)
    def _():
        keep_ref[...] = result


def direct_chunks(chunked, col_panel, ids, first, half, chunk_at):
    _, n_sub, _, _, sub_rows, width = chunked.shape
    n_blocks = col_panel.shape[0] // width
    group = math.gcd(n_blocks, 2)
    chunk_rows = n_sub * sub_rows // n_blocks

    def s_index(i, ids):
        qb, h, qs = chunk_at(ids[first + i])
        return (qb, 0, h, qs, 0, 0)

    out = jax.ShapeDtypeStruct((half * chunk_rows, width), F32)
    return pl.pallas_call(
        functools.partial(direct_body, n_blocks, group, half),
        grid_spec=pltpu.PrefetchScalarGridSpec(
            num_scalar_prefetch=1,
            grid=(2 * half,),
            in_specs=[
                pl.BlockSpec((None, n_sub, None, None, sub_rows, width), s_index),
                pl.BlockSpec((n_blocks * width, width), lambda i, ids: (0, 0)),
            ],
            out_specs=[
                pl.BlockSpec((chunk_rows, width), lambda i, ids: (jnp.minimum(i, half - 1), 0)),
                pl.BlockSpec((chunk_rows, width), lambda i, ids: (jnp.maximum(i - half, 0), 0)),
            ],
            scratch_shapes=[pltpu.VMEM((n_blocks // group, group * width, 2 * width), BF16)],
        ),
        out_shape=[out, out],
        compiler_params=pltpu.CompilerParams(vmem_limit_bytes=CHUNK_VMEM),
        cost_estimate=pl.CostEstimate(
            flops=12 * half * chunk_rows * n_blocks * width * width,
            bytes_accessed=8 * half * chunk_rows * n_blocks * width,
            transcendentals=0,
        ),
        name="direct",
    )(ids, chunked, col_panel)


def kept_body(first, half, high_ref, low_ref, p_ref, away_ref, keep_ref, right):
    step = pl.program_id(0)
    width = p_ref.shape[1]
    rows = away_ref.shape[0]

    @pl.when(step == 0)
    def _():
        high, low = split(p_ref[...])
        right[:, :width] = high
        right[:, width:] = low

    here = pl.ds(pl.multiple_of((first + step) * rows, rows), rows)
    both = dot(high_ref[here, :], right[...])
    result = both[:, :width] + both[:, width:] + dot(low_ref[here, :], right[:, :width])

    @pl.when(step < half)
    def _():
        away_ref[...] = result

    @pl.when(step >= half)
    def _():
        keep_ref[...] = result


def direct_kept(plan, high, low, col_panel, first, half):
    rows, width, depth = plan.chunk_rows, plan.width, col_panel.shape[0]
    out = jax.ShapeDtypeStruct((half * rows, width), F32)
    held = pl.BlockSpec(memory_space=pltpu.VMEM)
    return pl.pallas_call(
        functools.partial(kept_body, first, half),
        grid=(2 * half,),
        in_specs=[held, held, pl.BlockSpec((depth, width), lambda i: (0, 0))],
        out_specs=[
            pl.BlockSpec((rows, width), lambda i: (jnp.minimum(i, half - 1), 0)),
            pl.BlockSpec((rows, width), lambda i: (jnp.maximum(i - half, 0), 0)),
        ],
        out_shape=[out, out],
        scratch_shapes=[pltpu.VMEM((depth, 2 * width), BF16)],
        compiler_params=pltpu.CompilerParams(vmem_limit_bytes=DIRECT_VMEM),
        cost_estimate=pl.CostEstimate(
            flops=12 * half * rows * depth * width, bytes_accessed=8 * half * rows * width, transcendentals=0
        ),
        name="direct_kept",
    )(high, low, col_panel)


def solve_body(n_terms, ids_ref, *refs):
    terms, (inv_ref, b_ref, x_ref) = refs[:n_terms], refs[n_terms:]
    image = terms[0][...]
    for term in terms[1:]:
        image = image + term[...]
    total = b_ref[...].reshape(image.shape) - image
    x_ref[...] = full_dot(total, inv_ref[...])


def gram_body(ids_ref, x_ref, l_ref, g_ref):
    x = x_ref[...]
    g_ref[...] = -lax.dot_general(
        x, l_ref[...].reshape(x.shape), (((0,), (0,)), ((), ())), precision=HIGHEST, preferred_element_type=F32
    )


def on_my_chunk(plan, body, ids, inputs, laid_out, out_shape, name):
    _, n_sub, _, _, rows = plan.view

    def at(i, ids):
        b, h, s = plan.chunk_at(ids[plan.n_chunks - 1])
        return (b, 0, h, s, 0, 0)

    def whole(shape):
        return pl.BlockSpec(shape, lambda i, ids: (0, 0))

    return pl.pallas_call(
        body,
        grid_spec=pltpu.PrefetchScalarGridSpec(
            num_scalar_prefetch=1,
            grid=(1,),
            in_specs=[whole(x.shape) for x in inputs]
            + [pl.BlockSpec((None, n_sub, None, None, rows, plan.width), at)],
            out_specs=whole(out_shape),
        ),
        out_shape=jax.ShapeDtypeStruct(out_shape, F32),
        compiler_params=pltpu.CompilerParams(vmem_limit_bytes=SMALL_VMEM),
        name=name,
    )(ids, *inputs, laid_out.reshape(*plan.view, plan.width))


def place_body(plan, slots, has_base, ids_ref, *refs):
    out_ref, sems = refs[-2:]
    pieces = refs[1:-2] if has_base else refs[:-2]
    _, n_sub, _, _, rows = plan.view
    copies = []
    for k, (piece, slot) in enumerate(zip(pieces, slots)):
        b, h, s = plan.chunk_at(ids_ref[slot[0]])
        for i in range(n_sub):
            source = piece.at[pl.ds(i * rows, rows), :]
            copies.append(pltpu.make_async_copy(source, out_ref.at[b, i, h, s], sems.at[k, i]))
    for copy in copies:
        copy.start()
    for copy in copies:
        copy.wait()


def place(plan, base, pieces, slots, ids):
    _, n_sub, _, _, _ = plan.view
    anywhere = pl.BlockSpec(memory_space=pl.ANY)
    held = pl.BlockSpec(memory_space=pltpu.VMEM)
    bases = [] if base is None else [base]
    return pl.pallas_call(
        functools.partial(place_body, plan, [(slot,) for slot in slots], base is not None),
        grid_spec=pltpu.PrefetchScalarGridSpec(
            num_scalar_prefetch=1,
            grid=(1,),
            in_specs=[anywhere] * len(bases) + [held] * len(pieces),
            out_specs=anywhere,
            scratch_shapes=[pltpu.SemaphoreType.DMA((len(pieces), n_sub))],
        ),
        out_shape=jax.ShapeDtypeStruct((*plan.view, plan.width), F32),
        input_output_aliases={1: 0} if bases else {},
        compiler_params=pltpu.CompilerParams(vmem_limit_bytes=SMALL_VMEM),
        name="place",
    )(ids, *bases, *pieces)


class Plan:
    def __init__(self, n_row, n_col, col_blocks, width):
        self.n_row, self.n_chunks = n_row, n_col
        self.n_blocks, self.width = col_blocks, width
        self.group = math.gcd(col_blocks, 2)
        qb = min(n_row, col_blocks)
        self.qs = n_row // qb
        self.view = (qb, col_blocks // qb, n_col // n_row, self.qs, width // self.qs)
        self.chunk_rows = self.view[1] * self.view[4]
        self.pitch = col_blocks
        if col_blocks % 16 == 0:
            self.pitch = col_blocks + 8
        n_z = n_col // 2
        self.far = n_z // 2
        self.steps, self.offsets, self.twins = [], [], []
        for distance in range(self.far, -1, -1):
            here = sorted({distance % n_z, -distance % n_z})
            self.steps.append((len(self.offsets), here))
            self.offsets += here + here
            self.twins += [1] * len(here) + [0] * len(here)
        fits = KEEP_BYTES // (4 * self.chunk_rows * col_blocks * width)
        ends = [begin + 2 * len(here) for begin, here in self.steps]
        self.keep = max([end for end in ends if end <= fits], default=ends[0])
        self.skip = self.n_chunks - self.keep
        self.levels_per_step = -(-(width - 1).bit_length() // self.n_chunks)

    def chunk_at(self, chunk):
        h, q = chunk // self.n_row, chunk % self.n_row
        return q // self.qs, h, q % self.qs

    def flip_place(self, i):
        return (i + self.keep) % self.n_chunks


def per_device(trail_adjoint, panel, panel_adjoint, diag_block):
    width = diag_block.shape[0]
    n_row = lax.axis_size("row")
    n_col = lax.axis_size("col")
    ratio = n_col // n_row
    n_z = n_col // 2
    row_blocks = panel.shape[0]
    col_blocks = trail_adjoint.shape[2]
    plan = Plan(n_row, n_col, col_blocks, width)
    row_index = lax.axis_index("row")
    col_index = lax.axis_index("col")
    z, core = col_index // 2, col_index % 2
    move = functools.partial(send, n_row=n_row, n_col=n_col)
    up = lambda r, c: (r, (c + 2) % n_col)
    down = lambda r, c: (r, (c - 2) % n_col)
    twin = lambda r, c: (r, c ^ 1)
    ids = (z + jnp.array(plan.offsets, jnp.int32)) % n_z * 2 + (core ^ jnp.array(plan.twins, jnp.int32))

    def to_panel_user(r, c):
        h, s = divmod(c, n_row)
        return r ^ (((r ^ s) + 1) % n_row), h * n_row + r

    chosen = choose(panel.reshape(col_blocks, ratio, width, width), (col_index // n_row).reshape(1))
    col_panel = move(chosen.reshape(col_blocks * width, width), to_panel_user)

    parts, inv, high, low = flip_parts(plan, trail_adjoint, panel, diag_block, ids, row_index.reshape(1), n_row)
    flipped = parts[0]
    for k in range(1, n_row):
        flipped = flipped + move(parts[k], lambda r, c: (r ^ k, c))
    flipped = move(flipped, lambda r, c: (c % n_row, c // n_row * n_row + r))

    rows = plan.chunk_rows
    cut = rows // 2
    below, above, mine, after = None, None, None, None
    for begin, here in plan.steps:
        right, _ = lax.optimization_barrier((col_panel, after))
        if begin + 2 * len(here) <= plan.keep:
            away, keep = direct_kept(plan, high, low, right, begin, len(here))
        else:
            chunked = trail_adjoint.reshape(*plan.view[:4], plan.view[4] * col_blocks, width)
            away, keep = direct_chunks(chunked, right, ids, begin, len(here), plan.chunk_at)
        after = total = keep + move(away, twin)
        if here[0] == 0:
            mine = [total, below, above, flipped]
        elif len(here) == 1:
            below, above = move(total[:cut], up), move(total[cut:], down)
        else:
            first, second = total[:rows], total[rows:]
            if below.shape[0] == cut:
                first = jnp.concatenate([first[:cut] + below, first[cut:]], 0)
                second = jnp.concatenate([second[:cut], second[cut:] + above], 0)
            else:
                first, second = first + below, second + above
            below, above = move(first, up), move(second, down)

    x = on_my_chunk(
        plan, functools.partial(solve_body, len(mine)), ids, mine + [inv], panel_adjoint, (rows, width), "solve"
    )

    held = {0: x}
    below, above = x, x
    for distance in range(1, plan.far):
        below, above = move(below, up), move(above, down)
        held[-distance % n_z], held[distance] = below, above
    gram = on_my_chunk(plan, gram_body, ids, [x], panel, (width, width), "gram")
    gram = gram + sum(move(gram, lambda r, c: (r ^ k, c)) for k in range(1, n_row))
    other = {d: move(piece, twin) for d, piece in held.items()}
    halves = [move(below[:cut], up), move(above[cut:], down)]
    moving, total = gram, gram
    for _ in range(1, n_z):
        moving = move(moving, up)
        total = total + moving
    order = (z + jnp.arange(n_z, dtype=jnp.int32)) % n_z * 2
    place_ids = jnp.concatenate([order + core, order + (1 - core)])
    near = sorted(held)
    solved = place(
        plan, None, [held[d] for d in near] + [other[d] for d in near], near + [n_z + d for d in near], place_ids
    )
    last = jnp.concatenate(halves, 0)
    solved = place(plan, solved, [last, move(last, twin)], [plan.far, n_z + plan.far], place_ids)
    gram = total + move(total, twin)
    return (solved.reshape(row_blocks, width, width), jnp.tril(gram))


def solution(mesh):
    in_specs = (P(None, "row", None, "col"), P(None, "row", None), P(None, "row", None), P())
    out_specs = (P(None, "row", None), P())
    return jax.shard_map(
        per_device, mesh=mesh, in_specs=in_specs, out_specs=out_specs, check_vma=False
    )
```

```python
import functools
import math

import jax
import jax.numpy as jnp
from jax import lax
from jax.experimental import pallas as pl
from jax.experimental.pallas import tpu as pltpu
from jax.sharding import PartitionSpec as P

F32 = jnp.float32
BF16 = jnp.bfloat16
HIGHEST = lax.Precision.HIGHEST
AXES = ("row", "col")
KEEP_BYTES = 24 * 2**20
FLIP_VMEM = 20 * 2**20
DIRECT_VMEM = 12 * 2**20
CHUNK_VMEM = 24 * 2**20
SMALL_VMEM = 8 * 2**20
CHOOSE_VMEM = 60 * 2**20


def split(x):
    high = x.astype(BF16)
    return high, (x - high.astype(F32)).astype(BF16)


def dot(a, b):
    return jnp.dot(a, b, preferred_element_type=F32)


def full_dot(a, b):
    return jnp.dot(a, b, preferred_element_type=F32, precision=HIGHEST)


def send(x, target, n_row, n_col):
    pairs = []
    for r in range(n_row):
        for c in range(n_col):
            to_r, to_c = target(r, c)
            pairs.append((r * n_col + c, to_r * n_col + to_c))
    return lax.ppermute(x, AXES, pairs)


def choose(grouped, which):
    blocks, _, width, _ = grouped.shape

    def body(which_ref, source, target, sem):
        copy = pltpu.make_async_copy(source.at[:, which_ref[0]], target, sem)
        copy.start()
        copy.wait()

    return pl.pallas_call(
        body,
        grid_spec=pltpu.PrefetchScalarGridSpec(
            num_scalar_prefetch=1,
            grid=(1,),
            in_specs=[pl.BlockSpec(memory_space=pl.ANY)],
            out_specs=pl.BlockSpec(memory_space=pltpu.VMEM),
            scratch_shapes=[pltpu.SemaphoreType.DMA],
        ),
        out_shape=jax.ShapeDtypeStruct((blocks, width, width), F32),
        compiler_params=pltpu.CompilerParams(vmem_limit_bytes=CHOOSE_VMEM),
        name="choose",
    )(which, grouped)


def flip_body(plan, n_parts, me_ref, ids_ref, s_ref, l_ref, *refs):
    outs, (high_ref, low_ref, acc, turned, buf, sems) = refs[:n_parts], refs[n_parts:]
    step, n_steps, slot = pl.program_id(0), plan.n_chunks, pl.program_id(0) % 2
    n_blocks, rows, width = plan.n_blocks, plan.chunk_rows, plan.width

    def fetch(i, slot):
        qb, h, qs = plan.chunk_at(ids_ref[plan.n_chunks + i])
        target = buf.at[slot]
        if plan.pitch > n_blocks:
            target = target.at[:, :, pl.ds(0, n_blocks), :]
        return pltpu.make_async_copy(s_ref.at[qb, :, h, qs], target, sems.at[slot])

    @pl.when(step == 0)
    def _():
        fetch(0, 0).start()
        acc[...] = jnp.zeros_like(acc)

    @pl.when(step + 1 < n_steps)
    def _():
        fetch(step + 1, 1 - slot).start()

    l_high, l_low = split(l_ref[...].reshape(rows, width))
    left = jnp.concatenate([l_high, l_low], 1).T
    fetch(step, slot).wait()
    flat = buf.at[slot].reshape(rows * plan.pitch, width)
    kept = pl.ds(pl.multiple_of(jnp.maximum(step - plan.skip, 0) * rows, rows), rows)
    for first in range(0, n_blocks, plan.group):
        x = jnp.concatenate(
            [flat[pl.ds(b, rows, stride=plan.pitch), :] for b in range(first, first + plan.group)], 1
        )
        high, low = split(x)
        here = pl.ds(first * width, plan.group * width)
        high_ref[kept, here] = high
        low_ref[kept, here] = low
        both = dot(left, high)
        acc[:, here] += both[:width] + both[width:] + dot(left[:width], low)

    @pl.when(step == n_steps - 1)
    def _():
        for b in range(n_blocks):
            here = pl.ds(b * width, width)
            turned[here, :] = acc[:, here].T
        size = outs[0].shape[0]
        for k, out in enumerate(outs):
            start = pl.multiple_of((me_ref[0] ^ k) * size, size)
            out[...] = turned[pl.ds(start, size), :]


def flip_parts(plan, trail, panel, ids, me, n_row):
    width, n_blocks = plan.width, plan.n_blocks
    size = n_blocks * width // n_row
    kept = plan.keep * plan.chunk_rows
    qb, n_sub, ratio, qs, rows = plan.view
    if plan.pitch > n_blocks:
        source = trail.reshape(*plan.view, n_blocks, width)
        buffer = pltpu.VMEM((2, n_sub, rows, plan.pitch, width), F32)
    else:
        source = trail.reshape(*plan.view[:4], rows * n_blocks, width)
        buffer = pltpu.VMEM((2, n_sub, rows * n_blocks, width), F32)

    def l_index(i, me, ids):
        b, h, s = plan.chunk_at(ids[plan.n_chunks + i])
        return (b, 0, h, s, 0, 0)

    whole = pl.BlockSpec(memory_space=pltpu.VMEM)
    resident = pltpu.VMEM((kept, n_blocks * width), BF16)
    n = plan.n_chunks * plan.chunk_rows
    out = pl.pallas_call(
        functools.partial(flip_body, plan, n_row),
        grid_spec=pltpu.PrefetchScalarGridSpec(
            num_scalar_prefetch=2,
            grid=(plan.n_chunks,),
            in_specs=[
                pl.BlockSpec(memory_space=pl.ANY),
                pl.BlockSpec((None, n_sub, None, None, rows, width), l_index),
            ],
            out_specs=[pl.BlockSpec((size, width), lambda i, me, ids: (0, 0))] * n_row + [whole, whole],
            scratch_shapes=[
                pltpu.VMEM((width, n_blocks * width), F32),
                pltpu.VMEM((n_blocks * width, width), F32),
                buffer,
                pltpu.SemaphoreType.DMA((2,)),
            ],
        ),
        out_shape=[jax.ShapeDtypeStruct((size, width), F32)] * n_row
        + [resident, resident],
        compiler_params=pltpu.CompilerParams(vmem_limit_bytes=FLIP_VMEM),
        cost_estimate=pl.CostEstimate(
            flops=6 * n * n_blocks * width * width, bytes_accessed=4 * n * n_blocks * width, transcendentals=0
        ),
        name="flip",
    )(me, ids, source, panel.reshape(*plan.view, width))
    return out[:n_row], out[n_row], out[n_row + 1]


def direct_body(n_blocks, group, half, ids_ref, s_ref, p_ref, away_ref, keep_ref, right):
    step = pl.program_id(0)
    width = p_ref.shape[1]

    @pl.when(step == 0)
    def _():
        for g in range(n_blocks // group):
            high, low = split(p_ref[pl.ds(g * group * width, group * width), :])
            right[g, :, :width] = high
            right[g, :, width:] = low

    n_sub, sub_rows, _ = s_ref.shape
    rows = sub_rows // n_blocks

    def column(b):
        return jnp.concatenate([s_ref[i, pl.ds(b, rows, stride=n_blocks), :] for i in range(n_sub)], 0)

    both, rest = None, None
    for g in range(n_blocks // group):
        x = jnp.concatenate([column(g * group + b) for b in range(group)], 1)
        high, low = split(x)
        new_both = dot(high, right[g])
        new_rest = dot(low, right[g, :, :width])
        both = new_both if both is None else both + new_both
        rest = new_rest if rest is None else rest + new_rest
    result = both[:, :width] + both[:, width:] + rest

    @pl.when(step < half)
    def _():
        away_ref[...] = result

    @pl.when(step >= half)
    def _():
        keep_ref[...] = result


def direct_chunks(chunked, col_panel, ids, first, half, chunk_at):
    _, n_sub, _, _, sub_rows, width = chunked.shape
    n_blocks = col_panel.shape[0] // width
    group = math.gcd(n_blocks, 2)
    chunk_rows = n_sub * sub_rows // n_blocks

    def s_index(i, ids):
        qb, h, qs = chunk_at(ids[first + i])
        return (qb, 0, h, qs, 0, 0)

    out = jax.ShapeDtypeStruct((half * chunk_rows, width), F32)
    return pl.pallas_call(
        functools.partial(direct_body, n_blocks, group, half),
        grid_spec=pltpu.PrefetchScalarGridSpec(
            num_scalar_prefetch=1,
            grid=(2 * half,),
            in_specs=[
                pl.BlockSpec((None, n_sub, None, None, sub_rows, width), s_index),
                pl.BlockSpec((n_blocks * width, width), lambda i, ids: (0, 0)),
            ],
            out_specs=[
                pl.BlockSpec((chunk_rows, width), lambda i, ids: (jnp.minimum(i, half - 1), 0)),
                pl.BlockSpec((chunk_rows, width), lambda i, ids: (jnp.maximum(i - half, 0), 0)),
            ],
            scratch_shapes=[pltpu.VMEM((n_blocks // group, group * width, 2 * width), BF16)],
        ),
        out_shape=[out, out],
        compiler_params=pltpu.CompilerParams(vmem_limit_bytes=CHUNK_VMEM),
        cost_estimate=pl.CostEstimate(flops=1, bytes_accessed=1, transcendentals=0),
        name="direct",
    )(ids, chunked, col_panel)


def kept_body(first, half, high_ref, low_ref, p_ref, away_ref, keep_ref, right):
    step = pl.program_id(0)
    width = p_ref.shape[1]
    rows = away_ref.shape[0]

    @pl.when(step == 0)
    def _():
        high, low = split(p_ref[...])
        right[:, :width] = high
        right[:, width:] = low

    here = pl.ds(pl.multiple_of((first + step) * rows, rows), rows)
    both = dot(high_ref[here, :], right[...])
    result = both[:, :width] + both[:, width:] + dot(low_ref[here, :], right[:, :width])

    @pl.when(step < half)
    def _():
        away_ref[...] = result

    @pl.when(step >= half)
    def _():
        keep_ref[...] = result


def direct_kept(plan, high, low, col_panel, first, half):
    rows, width, depth = plan.chunk_rows, plan.width, col_panel.shape[0]
    out = jax.ShapeDtypeStruct((half * rows, width), F32)
    held = pl.BlockSpec(memory_space=pltpu.VMEM)
    return pl.pallas_call(
        functools.partial(kept_body, first, half),
        grid=(2 * half,),
        in_specs=[held, held, pl.BlockSpec((depth, width), lambda i: (0, 0))],
        out_specs=[
            pl.BlockSpec((rows, width), lambda i: (jnp.minimum(i, half - 1), 0)),
            pl.BlockSpec((rows, width), lambda i: (jnp.maximum(i - half, 0), 0)),
        ],
        out_shape=[out, out],
        scratch_shapes=[pltpu.VMEM((depth, 2 * width), BF16)],
        compiler_params=pltpu.CompilerParams(vmem_limit_bytes=DIRECT_VMEM),
        cost_estimate=pl.CostEstimate(flops=1, bytes_accessed=1, transcendentals=0),
        name="direct_kept",
    )(high, low, col_panel)


def inverse_body(d_ref, o_ref):
    d = d_ref[...]
    width = d.shape[0]
    i = lax.broadcasted_iota(jnp.int32, d.shape, 0)
    j = lax.broadcasted_iota(jnp.int32, d.shape, 1)
    inv = jnp.where(i == j, 1.0 / d, 0.0)
    level = 0
    while (1 << level) < width:
        same = (i >> (level + 1)) == (j >> (level + 1))
        below = (i >> level) > (j >> level)
        part = jnp.where(jnp.logical_and(same, below), d, 0.0)
        inv = inv - full_dot(inv, full_dot(part, inv))
        level += 1
    o_ref[...] = inv


def inverse(diag_block):
    return pl.pallas_call(
        inverse_body,
        out_shape=jax.ShapeDtypeStruct(diag_block.shape, F32),
        compiler_params=pltpu.CompilerParams(vmem_limit_bytes=SMALL_VMEM),
        name="inverse",
    )(diag_block)


def over_rows(a, b, **kwargs):
    return lax.dot_general(a, b, (((0,), (0,)), ((), ())), preferred_element_type=F32, **kwargs)


def moment_body(n_parts, ids_ref, me_ref, *refs):
    parts, (p_ref, b_ref, l_ref, out_ref) = refs[:n_parts], refs[n_parts:]
    size, width = parts[0].shape
    product = jnp.zeros((width, width), F32)
    for k, part in enumerate(parts):
        start = pl.multiple_of((me_ref[0] ^ k) * size, size)
        p_high, p_low = split(p_ref[pl.ds(start, size), :])
        f_high, f_low = split(part[...])
        product += over_rows(p_high, f_high) + over_rows(p_high, f_low) + over_rows(p_low, f_high)
    b = b_ref[...].reshape(-1, width)
    l = l_ref[...].reshape(-1, width)
    out_ref[...] = over_rows(b, l, precision=HIGHEST) - product - product.T


def moment(plan, parts, col_panel, given, panel, ids, me):
    _, n_sub, _, _, rows = plan.view
    width = plan.width

    def at(i, ids, me):
        b, h, s = plan.chunk_at(ids[plan.mine])
        return (b, 0, h, s, 0, 0)

    def whole(shape):
        return pl.BlockSpec(shape, lambda i, ids, me: (0, 0))

    chunk = pl.BlockSpec((None, n_sub, None, None, rows, width), at)
    return pl.pallas_call(
        functools.partial(moment_body, len(parts)),
        grid_spec=pltpu.PrefetchScalarGridSpec(
            num_scalar_prefetch=2,
            grid=(1,),
            in_specs=[whole(x.shape) for x in parts] + [whole(col_panel.shape), chunk, chunk],
            out_specs=whole((width, width)),
        ),
        out_shape=jax.ShapeDtypeStruct((width, width), F32),
        compiler_params=pltpu.CompilerParams(vmem_limit_bytes=DIRECT_VMEM),
        name="moment",
    )(ids, me, *parts, col_panel, given.reshape(*plan.view, width), panel.reshape(*plan.view, width))


def gram_body(inv_ref, moment_ref, g_ref):
    g = -over_rows(inv_ref[...], moment_ref[...], precision=HIGHEST)
    i = lax.broadcasted_iota(jnp.int32, g.shape, 0)
    j = lax.broadcasted_iota(jnp.int32, g.shape, 1)
    g_ref[...] = jnp.where(i >= j, g, 0.0)


def gram_of(inv, total):
    return pl.pallas_call(
        gram_body,
        out_shape=jax.ShapeDtypeStruct(inv.shape, F32),
        compiler_params=pltpu.CompilerParams(vmem_limit_bytes=SMALL_VMEM),
        name="gram",
    )(inv, total)


def solve_body(n_terms, ids_ref, *refs):
    terms, (inv_ref, b_ref, x_ref) = refs[:n_terms], refs[n_terms:]
    image = terms[0][...]
    for term in terms[1:]:
        image = image + term[...]
    total = b_ref[...].reshape(image.shape) - image
    x_ref[...] = full_dot(total, inv_ref[...])


def on_my_chunk(plan, body, ids, inputs, laid_out, out_shape, name):
    _, n_sub, _, _, rows = plan.view

    def at(i, ids):
        b, h, s = plan.chunk_at(ids[plan.mine])
        return (b, 0, h, s, 0, 0)

    def whole(shape):
        return pl.BlockSpec(shape, lambda i, ids: (0, 0))

    return pl.pallas_call(
        body,
        grid_spec=pltpu.PrefetchScalarGridSpec(
            num_scalar_prefetch=1,
            grid=(1,),
            in_specs=[whole(x.shape) for x in inputs]
            + [pl.BlockSpec((None, n_sub, None, None, rows, plan.width), at)],
            out_specs=whole(out_shape),
        ),
        out_shape=jax.ShapeDtypeStruct(out_shape, F32),
        compiler_params=pltpu.CompilerParams(vmem_limit_bytes=SMALL_VMEM),
        name=name,
    )(ids, *inputs, laid_out.reshape(*plan.view, plan.width))


def place_body(plan, slots, has_base, ids_ref, *refs):
    out_ref, sems = refs[-2:]
    pieces = refs[1:-2] if has_base else refs[:-2]
    _, n_sub, _, _, rows = plan.view
    copies = []
    for piece, (slot, half) in zip(pieces, slots):
        b, h, s = plan.chunk_at(ids_ref[slot])
        first, count = half * piece.shape[0], piece.shape[0]
        for i in range(n_sub):
            low, high = max(first, i * rows), min(first + count, (i + 1) * rows)
            if low < high:
                source = piece.at[pl.ds(low - first, high - low), :]
                target = out_ref.at[b, i, h, s, pl.ds(low - i * rows, high - low), :]
                copies.append(pltpu.make_async_copy(source, target, sems.at[len(copies)]))
    for copy in copies:
        copy.start()
    for copy in copies:
        copy.wait()


def place(plan, base, pieces, ids):
    anywhere = pl.BlockSpec(memory_space=pl.ANY)
    held = pl.BlockSpec(memory_space=pltpu.VMEM)
    bases = [] if base is None else [base]
    count = len(pieces) * (plan.view[1] + 1)
    return pl.pallas_call(
        functools.partial(place_body, plan, [piece[1:] for piece in pieces], base is not None),
        grid_spec=pltpu.PrefetchScalarGridSpec(
            num_scalar_prefetch=1,
            grid=(1,),
            in_specs=[anywhere] * len(bases) + [held] * len(pieces),
            out_specs=anywhere,
            scratch_shapes=[pltpu.SemaphoreType.DMA((count,))],
        ),
        out_shape=jax.ShapeDtypeStruct((*plan.view, plan.width), F32),
        input_output_aliases={1: 0} if bases else {},
        compiler_params=pltpu.CompilerParams(vmem_limit_bytes=SMALL_VMEM),
        name="place",
    )(ids, *bases, *[piece[0] for piece in pieces])


class Plan:
    def __init__(self, n_row, n_col, col_blocks, width):
        self.n_row, self.n_chunks = n_row, n_col
        self.n_blocks, self.width = col_blocks, width
        self.group = math.gcd(col_blocks, 2)
        qb = min(n_row, col_blocks)
        self.qs = n_row // qb
        self.view = (qb, col_blocks // qb, n_col // n_row, self.qs, width // self.qs)
        self.chunk_rows = self.view[1] * self.view[4]
        self.pitch = col_blocks
        if col_blocks % 16 == 0:
            self.pitch = col_blocks + 8
        n_z = n_col // 2
        self.far = n_z // 2
        self.steps, self.offsets, self.twins = [], [], []
        for distance in range(self.far, -1, -1):
            here = sorted({distance % n_z, -distance % n_z})
            self.steps.append((len(self.offsets), here))
            self.offsets += here + here
            if distance == 0:
                self.mine = len(self.offsets) - 1
            self.twins += [1] * len(here) + [0] * len(here)
        fits = KEEP_BYTES // (4 * self.chunk_rows * col_blocks * width)
        self.slots, held = {}, []
        for begin, here in sorted(self.steps, key=lambda step: step[1][0] == 0):
            places = range(begin, begin + 2 * len(here))
            if len(held) + len(places) <= fits:
                self.slots[begin] = len(held)
                held += places
        self.keep = len(held)
        self.skip = self.n_chunks - self.keep
        self.flip_order = [p for p in range(self.n_chunks) if p not in held] + held

    def chunk_at(self, chunk):
        h, q = chunk // self.n_row, chunk % self.n_row
        return q // self.qs, h, q % self.qs


def per_device(trail_adjoint, panel, panel_adjoint, diag_block):
    width = diag_block.shape[0]
    n_row = lax.axis_size("row")
    n_col = lax.axis_size("col")
    ratio = n_col // n_row
    n_z = n_col // 2
    row_blocks = panel.shape[0]
    col_blocks = trail_adjoint.shape[2]
    plan = Plan(n_row, n_col, col_blocks, width)
    row_index = lax.axis_index("row")
    col_index = lax.axis_index("col")
    z, core = col_index // 2, col_index % 2
    move = functools.partial(send, n_row=n_row, n_col=n_col)
    up = lambda r, c: (r, (c + 2) % n_col)
    down = lambda r, c: (r, (c - 2) % n_col)
    twin = lambda r, c: (r, c ^ 1)
    places = list(range(plan.n_chunks)) + plan.flip_order
    offsets = jnp.array([plan.offsets[p] for p in places], jnp.int32)
    twins = jnp.array([plan.twins[p] for p in places], jnp.int32)
    ids = (z + offsets) % n_z * 2 + (core ^ twins)

    def to_panel_user(r, c):
        h, s = divmod(c, n_row)
        return r ^ (((r ^ s) + 1) % n_row), h * n_row + r

    chosen = choose(panel.reshape(col_blocks, ratio, width, width), (col_index // n_row).reshape(1))
    col_panel = move(chosen.reshape(col_blocks * width, width), to_panel_user)

    me = row_index.reshape(1)
    parts, high, low = flip_parts(plan, trail_adjoint, panel, ids, me, n_row)
    arrived = [move(parts[k], lambda r, c: (r ^ k, c)) for k in range(1, n_row)]
    flip_sum = sum(arrived, parts[0])
    flipped = move(flip_sum, lambda r, c: (c % n_row, c // n_row * n_row + r))
    inv = inverse(diag_block)

    moments = [moment(plan, parts, col_panel, panel_adjoint, panel, ids, me)]
    bit = 1
    while bit < n_row:
        moments.append(moments[-1] + move(moments[-1], lambda r, c: (r ^ bit, c)))
        bit *= 2
    row_steps = len(moments) - 1

    rows = plan.chunk_rows
    cut = rows // 2
    below, above = None, None
    for begin, here in plan.steps:
        if here[0] == 0:
            fence = totals
        elif begin:
            fence = (keep, below, above, flip_sum)
        else:
            fence = inv
        right, _ = lax.optimization_barrier((col_panel, fence))
        if begin in plan.slots:
            away, keep = direct_kept(plan, high, low, right, plan.slots[begin], len(here))
        else:
            chunked = trail_adjoint.reshape(*plan.view[:4], plan.view[4] * col_blocks, width)
            away, keep = direct_chunks(chunked, right, ids, begin, len(here), plan.chunk_at)
        totals = []
        for k in range(len(here)):
            piece = slice(k * rows, (k + 1) * rows)
            totals.append(keep[piece] + move(away[piece], twin))
        if here[0] == 0:
            own = totals[0]
        elif len(here) == 1:
            below, above = move(totals[0][:cut], up), move(totals[0][cut:], down)
        else:
            first, second = totals
            if below.shape[0] == cut:
                first = jnp.concatenate([first[:cut] + below, first[cut:]], 0)
                second = jnp.concatenate([second[:cut], second[cut:] + above], 0)
            else:
                first, second = first + below, second + above
            below, above = move(first, up), move(second, down)
    mine = [own, below, above, flipped]

    bit = 1
    while bit < n_z:
        moments.append(moments[-1] + move(moments[-1], lambda r, c: (r, c ^ (2 * bit))))
        bit *= 2
    x = on_my_chunk(
        plan, functools.partial(solve_body, len(mine)), ids, mine + [inv], panel_adjoint, (rows, width), "solve"
    )

    lower, upper = {0: x[:cut]}, {0: x[cut:]}
    below, above = (x[:cut], x[cut:]), (x[cut:], x[:cut])
    for distance in range(1, plan.far):
        below, above = [move(b, up) for b in below], [move(a, down) for a in above]
        lower[-distance % n_z], upper[-distance % n_z] = below
        upper[distance], lower[distance] = above
    (go_up, go_down), _ = lax.optimization_barrier(((below[0], above[0]), moments[row_steps]))
    lower[plan.far], upper[plan.far] = move(go_up, up), move(go_down, down)
    order = (z + jnp.arange(n_z, dtype=jnp.int32)) % n_z * 2
    place_ids = jnp.concatenate([order + core, order + (1 - core)])
    near = [d for d in range(n_z) if d != plan.far]
    pieces = [(lower[d], d, 0) for d in near] + [(upper[d], d, 1) for d in near]
    pieces += [(move(piece, twin), n_z + d, half) for piece, d, half in pieces]
    solved = place(plan, None, pieces, place_ids)
    gram = gram_of(inv, moments[-1] + move(moments[-1], twin))
    (lower[plan.far], upper[plan.far]), (solved, gram) = lax.optimization_barrier(
        ((lower[plan.far], upper[plan.far]), (solved, gram))
    )
    last = [(lower[plan.far], plan.far, 0), (upper[plan.far], plan.far, 1)]
    last += [(move(piece, twin), n_z + d, half) for piece, d, half in last]
    solved = place(plan, solved, last, place_ids)
    return solved.reshape(row_blocks, width, width), gram


def solution(mesh):
    in_specs = (P(None, "row", None, "col"), P(None, "row", None), P(None, "row", None), P())
    out_specs = (P(None, "row", None), P())
    return jax.shard_map(
        per_device, mesh=mesh, in_specs=in_specs, out_specs=out_specs, check_vma=False
    )
```

```python
import functools
import math

import jax
import jax.numpy as jnp
from jax import lax
from jax.experimental import pallas as pl
from jax.experimental.pallas import tpu as pltpu
from jax.sharding import PartitionSpec as P

F32 = jnp.float32
BF16 = jnp.bfloat16
HIGHEST = lax.Precision.HIGHEST
AXES = ("row", "col")
KEEP_BYTES = 24 * 2**20
FLIP_VMEM = 20 * 2**20
DIRECT_VMEM = 12 * 2**20
CHUNK_VMEM = 24 * 2**20
SMALL_VMEM = 8 * 2**20
CHOOSE_VMEM = 60 * 2**20


def split(x):
    high = x.astype(BF16)
    return high, (x - high.astype(F32)).astype(BF16)


def dot(a, b):
    return jnp.dot(a, b, preferred_element_type=F32)


def full_dot(a, b):
    return jnp.dot(a, b, preferred_element_type=F32, precision=HIGHEST)


def send(x, target, n_row, n_col):
    pairs = []
    for r in range(n_row):
        for c in range(n_col):
            to_r, to_c = target(r, c)
            pairs.append((r * n_col + c, to_r * n_col + to_c))
    return lax.ppermute(x, AXES, pairs)


def choose(grouped, which):
    blocks, _, width, _ = grouped.shape

    def body(which_ref, source, target, sem):
        copy = pltpu.make_async_copy(source.at[:, which_ref[0]], target, sem)
        copy.start()
        copy.wait()

    return pl.pallas_call(
        body,
        grid_spec=pltpu.PrefetchScalarGridSpec(
            num_scalar_prefetch=1,
            grid=(1,),
            in_specs=[pl.BlockSpec(memory_space=pl.ANY)],
            out_specs=pl.BlockSpec(memory_space=pltpu.VMEM),
            scratch_shapes=[pltpu.SemaphoreType.DMA],
        ),
        out_shape=jax.ShapeDtypeStruct((blocks, width, width), F32),
        compiler_params=pltpu.CompilerParams(vmem_limit_bytes=CHOOSE_VMEM),
        name="choose",
    )(which, grouped)


def flip_body(plan, n_parts, me_ref, ids_ref, s_ref, l_ref, *refs):
    outs, (high_ref, low_ref, acc, turned, buf, sems) = refs[:n_parts], refs[n_parts:]
    step, n_steps, slot = pl.program_id(0), plan.n_chunks, pl.program_id(0) % 2
    n_blocks, rows, width = plan.n_blocks, plan.chunk_rows, plan.width

    def fetch(i, slot):
        qb, h, qs = plan.chunk_at(ids_ref[plan.n_chunks + i])
        target = buf.at[slot]
        if plan.pitch > n_blocks:
            target = target.at[:, :, pl.ds(0, n_blocks), :]
        return pltpu.make_async_copy(s_ref.at[qb, :, h, qs], target, sems.at[slot])

    @pl.when(step == 0)
    def _():
        fetch(0, 0).start()
        acc[...] = jnp.zeros_like(acc)

    @pl.when(step + 1 < n_steps)
    def _():
        fetch(step + 1, 1 - slot).start()

    l_high, l_low = split(l_ref[...].reshape(rows, width))
    left = jnp.concatenate([l_high, l_low], 1).T
    fetch(step, slot).wait()
    flat = buf.at[slot].reshape(rows * plan.pitch, width)
    kept = pl.ds(pl.multiple_of(jnp.maximum(step - plan.skip, 0) * rows, rows), rows)
    for first in range(0, n_blocks, plan.group):
        x = jnp.concatenate(
            [flat[pl.ds(b, rows, stride=plan.pitch), :] for b in range(first, first + plan.group)], 1
        )
        high, low = split(x)
        here = pl.ds(first * width, plan.group * width)
        high_ref[kept, here] = high
        low_ref[kept, here] = low
        both = dot(left, high)
        acc[:, here] += both[:width] + both[width:] + dot(left[:width], low)

    @pl.when(step == n_steps - 1)
    def _():
        for b in range(n_blocks):
            here = pl.ds(b * width, width)
            turned[here, :] = acc[:, here].T
        size = outs[0].shape[0]
        for k, out in enumerate(outs):
            start = pl.multiple_of((me_ref[0] ^ k) * size, size)
            out[...] = turned[pl.ds(start, size), :]


def flip_parts(plan, trail, panel, ids, me, n_row):
    width, n_blocks = plan.width, plan.n_blocks
    size = n_blocks * width // n_row
    kept = plan.keep * plan.chunk_rows
    qb, n_sub, ratio, qs, rows = plan.view
    if plan.pitch > n_blocks:
        source = trail.reshape(*plan.view, n_blocks, width)
        buffer = pltpu.VMEM((2, n_sub, rows, plan.pitch, width), F32)
    else:
        source = trail.reshape(*plan.view[:4], rows * n_blocks, width)
        buffer = pltpu.VMEM((2, n_sub, rows * n_blocks, width), F32)

    def l_index(i, me, ids):
        b, h, s = plan.chunk_at(ids[plan.n_chunks + i])
        return (b, 0, h, s, 0, 0)

    whole = pl.BlockSpec(memory_space=pltpu.VMEM)
    resident = pltpu.VMEM((kept, n_blocks * width), BF16)
    n = plan.n_chunks * plan.chunk_rows
    out = pl.pallas_call(
        functools.partial(flip_body, plan, n_row),
        grid_spec=pltpu.PrefetchScalarGridSpec(
            num_scalar_prefetch=2,
            grid=(plan.n_chunks,),
            in_specs=[
                pl.BlockSpec(memory_space=pl.ANY),
                pl.BlockSpec((None, n_sub, None, None, rows, width), l_index),
            ],
            out_specs=[pl.BlockSpec((size, width), lambda i, me, ids: (0, 0))] * n_row + [whole, whole],
            scratch_shapes=[
                pltpu.VMEM((width, n_blocks * width), F32),
                pltpu.VMEM((n_blocks * width, width), F32),
                buffer,
                pltpu.SemaphoreType.DMA((2,)),
            ],
        ),
        out_shape=[jax.ShapeDtypeStruct((size, width), F32)] * n_row
        + [resident, resident],
        compiler_params=pltpu.CompilerParams(vmem_limit_bytes=FLIP_VMEM),
        cost_estimate=pl.CostEstimate(
            flops=6 * n * n_blocks * width * width, bytes_accessed=4 * n * n_blocks * width, transcendentals=0
        ),
        name="flip",
    )(me, ids, source, panel.reshape(*plan.view, width))
    return out[:n_row], out[n_row], out[n_row + 1]


def direct_body(n_blocks, group, half, ids_ref, s_ref, p_ref, *refs):
    away_ref, keep_ref, right = refs[-3:]
    step = pl.program_id(0)
    width = p_ref.shape[1]

    @pl.when(step == 0)
    def _():
        for g in range(n_blocks // group):
            high, low = split(p_ref[pl.ds(g * group * width, group * width), :])
            right[g, :, :width] = high
            right[g, :, width:] = low

    n_sub, sub_rows, _ = s_ref.shape
    rows = sub_rows // n_blocks

    def column(b):
        return jnp.concatenate([s_ref[i, pl.ds(b, rows, stride=n_blocks), :] for i in range(n_sub)], 0)

    both, rest = None, None
    for g in range(n_blocks // group):
        x = jnp.concatenate([column(g * group + b) for b in range(group)], 1)
        high, low = split(x)
        new_both = dot(high, right[g])
        new_rest = dot(low, right[g, :, :width])
        both = new_both if both is None else both + new_both
        rest = new_rest if rest is None else rest + new_rest
    result = both[:, :width] + both[:, width:] + rest

    @pl.when(step < half)
    def _():
        away_ref[...] = result

    @pl.when(step >= half)
    def _():
        keep_ref[...] = result


def direct_chunks(chunked, col_panel, ids, first, half, chunk_at, earlier=()):
    _, n_sub, _, _, sub_rows, width = chunked.shape
    n_blocks = col_panel.shape[0] // width
    group = math.gcd(n_blocks, 2)
    chunk_rows = n_sub * sub_rows // n_blocks

    def s_index(i, ids):
        qb, h, qs = chunk_at(ids[first + i])
        return (qb, 0, h, qs, 0, 0)

    out = jax.ShapeDtypeStruct((half * chunk_rows, width), F32)
    return pl.pallas_call(
        functools.partial(direct_body, n_blocks, group, half),
        grid_spec=pltpu.PrefetchScalarGridSpec(
            num_scalar_prefetch=1,
            grid=(2 * half,),
            in_specs=[
                pl.BlockSpec((None, n_sub, None, None, sub_rows, width), s_index),
                pl.BlockSpec((n_blocks * width, width), lambda i, ids: (0, 0)),
            ]
            + [pl.BlockSpec(memory_space=pl.ANY)] * len(earlier),
            out_specs=[
                pl.BlockSpec((chunk_rows, width), lambda i, ids: (jnp.minimum(i, half - 1), 0)),
                pl.BlockSpec((chunk_rows, width), lambda i, ids: (jnp.maximum(i - half, 0), 0)),
            ],
            scratch_shapes=[pltpu.VMEM((n_blocks // group, group * width, 2 * width), BF16)],
        ),
        out_shape=[out, out],
        compiler_params=pltpu.CompilerParams(vmem_limit_bytes=CHUNK_VMEM),
        cost_estimate=pl.CostEstimate(flops=1, bytes_accessed=1, transcendentals=0),
        name="direct",
    )(ids, chunked, col_panel, *earlier)


def kept_body(first, half, high_ref, low_ref, p_ref, *refs):
    away_ref, keep_ref, right = refs[-3:]
    step = pl.program_id(0)
    width = p_ref.shape[1]
    rows = away_ref.shape[0]

    @pl.when(step == 0)
    def _():
        high, low = split(p_ref[...])
        right[:, :width] = high
        right[:, width:] = low

    here = pl.ds(pl.multiple_of((first + step) * rows, rows), rows)
    both = dot(high_ref[here, :], right[...])
    result = both[:, :width] + both[:, width:] + dot(low_ref[here, :], right[:, :width])

    @pl.when(step < half)
    def _():
        away_ref[...] = result

    @pl.when(step >= half)
    def _():
        keep_ref[...] = result


def direct_kept(plan, high, low, col_panel, first, half, earlier=()):
    rows, width, depth = plan.chunk_rows, plan.width, col_panel.shape[0]
    out = jax.ShapeDtypeStruct((half * rows, width), F32)
    held = pl.BlockSpec(memory_space=pltpu.VMEM)
    return pl.pallas_call(
        functools.partial(kept_body, first, half),
        grid=(2 * half,),
        in_specs=[held, held, pl.BlockSpec((depth, width), lambda i: (0, 0))]
        + [pl.BlockSpec(memory_space=pl.ANY)] * len(earlier),
        out_specs=[
            pl.BlockSpec((rows, width), lambda i: (jnp.minimum(i, half - 1), 0)),
            pl.BlockSpec((rows, width), lambda i: (jnp.maximum(i - half, 0), 0)),
        ],
        out_shape=[out, out],
        scratch_shapes=[pltpu.VMEM((depth, 2 * width), BF16)],
        compiler_params=pltpu.CompilerParams(vmem_limit_bytes=DIRECT_VMEM),
        cost_estimate=pl.CostEstimate(flops=1, bytes_accessed=1, transcendentals=0),
        name="direct_kept",
    )(high, low, col_panel, *earlier)


def inverse_body(d_ref, o_ref):
    d = d_ref[...]
    width = d.shape[0]
    i = lax.broadcasted_iota(jnp.int32, d.shape, 0)
    j = lax.broadcasted_iota(jnp.int32, d.shape, 1)
    inv = jnp.where(i == j, 1.0 / d, 0.0)
    level = 0
    while (1 << level) < width:
        same = (i >> (level + 1)) == (j >> (level + 1))
        below = (i >> level) > (j >> level)
        part = jnp.where(jnp.logical_and(same, below), d, 0.0)
        inv = inv - full_dot(inv, full_dot(part, inv))
        level += 1
    o_ref[...] = inv


def inverse(diag_block):
    return pl.pallas_call(
        inverse_body,
        out_shape=jax.ShapeDtypeStruct(diag_block.shape, F32),
        compiler_params=pltpu.CompilerParams(vmem_limit_bytes=SMALL_VMEM),
        name="inverse",
    )(diag_block)


def over_rows(a, b, **kwargs):
    return lax.dot_general(a, b, (((0,), (0,)), ((), ())), preferred_element_type=F32, **kwargs)


def moment_body(n_parts, ids_ref, me_ref, *refs):
    parts, (p_ref, b_ref, l_ref, out_ref) = refs[:n_parts], refs[n_parts:]
    size, width = parts[0].shape
    product = jnp.zeros((width, width), F32)
    for k, part in enumerate(parts):
        start = pl.multiple_of((me_ref[0] ^ k) * size, size)
        p_high, p_low = split(p_ref[pl.ds(start, size), :])
        f_high, f_low = split(part[...])
        product += over_rows(p_high, f_high) + over_rows(p_high, f_low) + over_rows(p_low, f_high)
    b = b_ref[...].reshape(-1, width)
    l = l_ref[...].reshape(-1, width)
    out_ref[...] = over_rows(b, l, precision=HIGHEST) - product - product.T


def moment(plan, parts, col_panel, given, panel, ids, me):
    _, n_sub, _, _, rows = plan.view
    width = plan.width

    def at(i, ids, me):
        b, h, s = plan.chunk_at(ids[plan.mine])
        return (b, 0, h, s, 0, 0)

    def whole(shape):
        return pl.BlockSpec(shape, lambda i, ids, me: (0, 0))

    chunk = pl.BlockSpec((None, n_sub, None, None, rows, width), at)
    return pl.pallas_call(
        functools.partial(moment_body, len(parts)),
        grid_spec=pltpu.PrefetchScalarGridSpec(
            num_scalar_prefetch=2,
            grid=(1,),
            in_specs=[whole(x.shape) for x in parts] + [whole(col_panel.shape), chunk, chunk],
            out_specs=whole((width, width)),
        ),
        out_shape=jax.ShapeDtypeStruct((width, width), F32),
        compiler_params=pltpu.CompilerParams(vmem_limit_bytes=DIRECT_VMEM),
        name="moment",
    )(ids, me, *parts, col_panel, given.reshape(*plan.view, width), panel.reshape(*plan.view, width))


def gram_body(inv_ref, moment_ref, g_ref):
    g = -over_rows(inv_ref[...], moment_ref[...], precision=HIGHEST)
    i = lax.broadcasted_iota(jnp.int32, g.shape, 0)
    j = lax.broadcasted_iota(jnp.int32, g.shape, 1)
    g_ref[...] = jnp.where(i >= j, g, 0.0)


def gram_of(inv, total):
    return pl.pallas_call(
        gram_body,
        out_shape=jax.ShapeDtypeStruct(inv.shape, F32),
        compiler_params=pltpu.CompilerParams(vmem_limit_bytes=SMALL_VMEM),
        name="gram",
    )(inv, total)


def solve_body(n_terms, ids_ref, *refs):
    terms, inv_ref, b_ref, x_ref = refs[:n_terms], refs[n_terms], refs[-2], refs[-1]
    image = terms[0][...]
    for term in terms[1:]:
        image = image + term[...]
    total = b_ref[...].reshape(image.shape) - image
    x_ref[...] = full_dot(total, inv_ref[...])


def on_my_chunk(plan, body, ids, inputs, laid_out, out_shape, name):
    _, n_sub, _, _, rows = plan.view

    def at(i, ids):
        b, h, s = plan.chunk_at(ids[plan.mine])
        return (b, 0, h, s, 0, 0)

    def whole(shape):
        return pl.BlockSpec(shape, lambda i, ids: (0, 0))

    return pl.pallas_call(
        body,
        grid_spec=pltpu.PrefetchScalarGridSpec(
            num_scalar_prefetch=1,
            grid=(1,),
            in_specs=[whole(x.shape) for x in inputs]
            + [pl.BlockSpec((None, n_sub, None, None, rows, plan.width), at)],
            out_specs=whole(out_shape),
        ),
        out_shape=jax.ShapeDtypeStruct(out_shape, F32),
        compiler_params=pltpu.CompilerParams(vmem_limit_bytes=SMALL_VMEM),
        name=name,
    )(ids, *inputs, laid_out.reshape(*plan.view, plan.width))


def place_body(plan, slots, has_base, ids_ref, *refs):
    out_ref, sems = refs[-2:]
    pieces = refs[1:-2] if has_base else refs[:-2]
    _, n_sub, _, _, rows = plan.view
    copies = []
    for piece, (slot, half) in zip(pieces, slots):
        b, h, s = plan.chunk_at(ids_ref[slot])
        first, count = half * piece.shape[0], piece.shape[0]
        for i in range(n_sub):
            low, high = max(first, i * rows), min(first + count, (i + 1) * rows)
            if low < high:
                source = piece.at[pl.ds(low - first, high - low), :]
                target = out_ref.at[b, i, h, s, pl.ds(low - i * rows, high - low), :]
                copies.append(pltpu.make_async_copy(source, target, sems.at[len(copies)]))
    for copy in copies:
        copy.start()
    for copy in copies:
        copy.wait()


def place(plan, base, pieces, ids):
    anywhere = pl.BlockSpec(memory_space=pl.ANY)
    held = pl.BlockSpec(memory_space=pltpu.VMEM)
    bases = [] if base is None else [base]
    count = len(pieces) * (plan.view[1] + 1)
    return pl.pallas_call(
        functools.partial(place_body, plan, [piece[1:] for piece in pieces], base is not None),
        grid_spec=pltpu.PrefetchScalarGridSpec(
            num_scalar_prefetch=1,
            grid=(1,),
            in_specs=[anywhere] * len(bases) + [held] * len(pieces),
            out_specs=anywhere,
            scratch_shapes=[pltpu.SemaphoreType.DMA((count,))],
        ),
        out_shape=jax.ShapeDtypeStruct((*plan.view, plan.width), F32),
        input_output_aliases={1: 0} if bases else {},
        compiler_params=pltpu.CompilerParams(vmem_limit_bytes=SMALL_VMEM),
        name="place",
    )(ids, *bases, *[piece[0] for piece in pieces])


class Plan:
    def __init__(self, n_row, n_col, col_blocks, width):
        self.n_row, self.n_chunks = n_row, n_col
        self.n_blocks, self.width = col_blocks, width
        self.group = math.gcd(col_blocks, 2)
        qb = min(n_row, col_blocks)
        self.qs = n_row // qb
        self.view = (qb, col_blocks // qb, n_col // n_row, self.qs, width // self.qs)
        self.chunk_rows = self.view[1] * self.view[4]
        self.pitch = col_blocks
        if col_blocks % 16 == 0:
            self.pitch = col_blocks + 8
        n_z = n_col // 2
        self.far = n_z // 2
        self.steps, self.offsets, self.twins = [], [], []
        for distance in range(self.far, -1, -1):
            here = sorted({distance % n_z, -distance % n_z})
            self.steps.append((len(self.offsets), here))
            self.offsets += here + here
            if distance == 0:
                self.mine = len(self.offsets) - 1
            self.twins += [1] * len(here) + [0] * len(here)
        fits = KEEP_BYTES // (4 * self.chunk_rows * col_blocks * width)
        self.slots, held = {}, []
        for begin, here in sorted(self.steps, key=lambda step: step[1][0] == 0):
            places = range(begin, begin + 2 * len(here))
            if len(held) + len(places) <= fits:
                self.slots[begin] = len(held)
                held += places
        self.keep = len(held)
        self.skip = self.n_chunks - self.keep
        self.flip_order = [p for p in range(self.n_chunks) if p not in held] + held

    def chunk_at(self, chunk):
        h, q = chunk // self.n_row, chunk % self.n_row
        return q // self.qs, h, q % self.qs


def per_device(trail_adjoint, panel, panel_adjoint, diag_block):
    width = diag_block.shape[0]
    n_row = lax.axis_size("row")
    n_col = lax.axis_size("col")
    ratio = n_col // n_row
    n_z = n_col // 2
    row_blocks = panel.shape[0]
    col_blocks = trail_adjoint.shape[2]
    plan = Plan(n_row, n_col, col_blocks, width)
    row_index = lax.axis_index("row")
    col_index = lax.axis_index("col")
    z, core = col_index // 2, col_index % 2
    move = functools.partial(send, n_row=n_row, n_col=n_col)
    up = lambda r, c: (r, (c + 2) % n_col)
    down = lambda r, c: (r, (c - 2) % n_col)
    twin = lambda r, c: (r, c ^ 1)
    places = list(range(plan.n_chunks)) + plan.flip_order
    offsets = jnp.array([plan.offsets[p] for p in places], jnp.int32)
    twins = jnp.array([plan.twins[p] for p in places], jnp.int32)
    ids = (z + offsets) % n_z * 2 + (core ^ twins)

    def to_panel_user(r, c):
        h, s = divmod(c, n_row)
        return r ^ (((r ^ s) + 1) % n_row), h * n_row + r

    chosen = choose(panel.reshape(col_blocks, ratio, width, width), (col_index // n_row).reshape(1))
    col_panel = move(chosen.reshape(col_blocks * width, width), to_panel_user)

    me = row_index.reshape(1)
    parts, high, low = flip_parts(plan, trail_adjoint, panel, ids, me, n_row)
    arrived = [move(parts[k], lambda r, c: (r ^ k, c)) for k in range(1, n_row)]
    flip_sum = sum(arrived, parts[0])
    flipped = move(flip_sum, lambda r, c: (c % n_row, c // n_row * n_row + r))
    inv = inverse(diag_block)

    moments = [moment(plan, parts, col_panel, panel_adjoint, panel, ids, me)]
    bit = 1
    while bit < n_row:
        moments.append(moments[-1] + move(moments[-1], lambda r, c: (r ^ bit, c)))
        bit *= 2
    row_steps = len(moments) - 1

    def later(*arrays, times=1):
        few = sum(x[:8] for x in arrays)
        for _ in range(times):
            few = move(few, twin)
        return few

    rows = plan.chunk_rows
    cut = rows // 2
    sent = []
    for begin, here in plan.steps:
        if here[0] == 0:
            earlier = totals
        elif begin:
            earlier = totals + [flip_sum, moments[1]]
        else:
            earlier = [inv]
        right = col_panel
        if begin in plan.slots:
            away, keep = direct_kept(plan, high, low, right, plan.slots[begin], len(here), earlier)
        else:
            chunked = trail_adjoint.reshape(*plan.view[:4], plan.view[4] * col_blocks, width)
            away, keep = direct_chunks(chunked, right, ids, begin, len(here), plan.chunk_at, earlier)
        totals = []
        for k in range(len(here)):
            piece = slice(k * rows, (k + 1) * rows)
            totals.append(keep[piece] + move(away[piece], twin))
        if here[0] == 0:
            own = totals[0]
        else:
            sent += [
                move(total, lambda r, c: (r, (c + 2 * distance) % n_col)) for distance, total in zip(here, totals)
            ]
    mine = [own, flipped] + sent

    bit = 1
    while bit < n_z:
        moments.append(moments[-1] + move(moments[-1], lambda r, c: (r, c ^ (2 * bit))))
        bit *= 2
    x = on_my_chunk(
        plan, functools.partial(solve_body, len(mine)), ids, mine + [inv] + [later(*sent)], panel_adjoint, (rows, width), "solve"
    )

    lower, upper = {0: x[:cut]}, {0: x[cut:]}
    below, above = (x[:cut], x[cut:]), (x[cut:], x[:cut])
    for distance in range(1, plan.far):
        below, above = [move(b, up) for b in below], [move(a, down) for a in above]
        lower[-distance % n_z], upper[-distance % n_z] = below
        upper[distance], lower[distance] = above
    (go_up, go_down), _ = lax.optimization_barrier(((below[0], above[0]), moments[row_steps]))
    lower[plan.far], upper[plan.far] = move(go_up, up), move(go_down, down)
    order = (z + jnp.arange(n_z, dtype=jnp.int32)) % n_z * 2
    place_ids = jnp.concatenate([order + core, order + (1 - core)])
    near = [d for d in range(n_z) if d != plan.far]
    pieces = [(lower[d], d, 0) for d in near] + [(upper[d], d, 1) for d in near]
    pieces += [(move(piece, twin), n_z + d, half) for piece, d, half in pieces]
    solved = place(plan, None, pieces, place_ids)
    gram = gram_of(inv, moments[-1] + move(moments[-1], twin))
    (lower[plan.far], upper[plan.far]), (solved, gram) = lax.optimization_barrier(
        ((lower[plan.far], upper[plan.far]), (solved, gram))
    )
    last = [(lower[plan.far], plan.far, 0), (upper[plan.far], plan.far, 1)]
    last += [(move(piece, twin), n_z + d, half) for piece, d, half in last]
    solved = place(plan, solved, last, place_ids)
    return solved.reshape(row_blocks, width, width), gram


def solution(mesh):
    in_specs = (P(None, "row", None, "col"), P(None, "row", None), P(None, "row", None), P())
    out_specs = (P(None, "row", None), P())
    return jax.shard_map(
        per_device, mesh=mesh, in_specs=in_specs, out_specs=out_specs, check_vma=False
    )
```

```python
import functools
import math

import jax
import jax.numpy as jnp
from jax import lax
from jax.experimental import pallas as pl
from jax.experimental.pallas import tpu as pltpu
from jax.sharding import PartitionSpec as P

F32 = jnp.float32
BF16 = jnp.bfloat16
HIGHEST = lax.Precision.HIGHEST
AXES = ("row", "col")
KEEP_BYTES = 24 * 2**20
FLIP_VMEM = 20 * 2**20
DIRECT_VMEM = 12 * 2**20
CHUNK_VMEM = 24 * 2**20
SMALL_VMEM = 8 * 2**20
CHOOSE_VMEM = 60 * 2**20


def split(x):
    high = x.astype(BF16)
    return high, (x - high.astype(F32)).astype(BF16)


def dot(a, b):
    return jnp.dot(a, b, preferred_element_type=F32)


def full_dot(a, b):
    return jnp.dot(a, b, preferred_element_type=F32, precision=HIGHEST)


def send(x, target, n_row, n_col):
    pairs = []
    for r in range(n_row):
        for c in range(n_col):
            to_r, to_c = target(r, c)
            pairs.append((r * n_col + c, to_r * n_col + to_c))
    return lax.ppermute(x, AXES, pairs)


def choose(grouped, which):
    blocks, _, width, _ = grouped.shape

    def body(which_ref, source, target, sem):
        copy = pltpu.make_async_copy(source.at[:, which_ref[0]], target, sem)
        copy.start()
        copy.wait()

    return pl.pallas_call(
        body,
        grid_spec=pltpu.PrefetchScalarGridSpec(
            num_scalar_prefetch=1,
            grid=(1,),
            in_specs=[pl.BlockSpec(memory_space=pl.ANY)],
            out_specs=pl.BlockSpec(memory_space=pltpu.VMEM),
            scratch_shapes=[pltpu.SemaphoreType.DMA],
        ),
        out_shape=jax.ShapeDtypeStruct((blocks, width, width), F32),
        compiler_params=pltpu.CompilerParams(vmem_limit_bytes=CHOOSE_VMEM),
        name="choose",
    )(which, grouped)


def flip_body(plan, n_parts, me_ref, ids_ref, s_ref, l_ref, *refs):
    outs, (high_ref, low_ref, acc, turned, buf, sems) = refs[:n_parts], refs[n_parts:]
    step, n_steps, slot = pl.program_id(0), plan.n_chunks, pl.program_id(0) % 2
    n_blocks, rows, width = plan.n_blocks, plan.chunk_rows, plan.width

    def fetch(i, slot):
        qb, h, qs = plan.chunk_at(ids_ref[plan.n_chunks + i])
        target = buf.at[slot]
        if plan.pitch > n_blocks:
            target = target.at[:, :, pl.ds(0, n_blocks), :]
        return pltpu.make_async_copy(s_ref.at[qb, :, h, qs], target, sems.at[slot])

    @pl.when(step == 0)
    def _():
        fetch(0, 0).start()
        acc[...] = jnp.zeros_like(acc)

    @pl.when(step + 1 < n_steps)
    def _():
        fetch(step + 1, 1 - slot).start()

    l_high, l_low = split(l_ref[...].reshape(rows, width))
    left = jnp.concatenate([l_high, l_low], 1).T
    fetch(step, slot).wait()
    flat = buf.at[slot].reshape(rows * plan.pitch, width)
    kept = pl.ds(pl.multiple_of(jnp.maximum(step - plan.skip, 0) * rows, rows), rows)
    for first in range(0, n_blocks, plan.group):
        x = jnp.concatenate(
            [flat[pl.ds(b, rows, stride=plan.pitch), :] for b in range(first, first + plan.group)], 1
        )
        high, low = split(x)
        here = pl.ds(first * width, plan.group * width)
        high_ref[kept, here] = high
        low_ref[kept, here] = low
        both = dot(left, high)
        acc[:, here] += both[:width] + both[width:] + dot(left[:width], low)

    @pl.when(step == n_steps - 1)
    def _():
        for b in range(n_blocks):
            here = pl.ds(b * width, width)
            turned[here, :] = acc[:, here].T
        size = outs[0].shape[0]
        for k, out in enumerate(outs):
            start = pl.multiple_of((me_ref[0] ^ k) * size, size)
            out[...] = turned[pl.ds(start, size), :]


def flip_parts(plan, trail, panel, ids, me, n_row):
    width, n_blocks = plan.width, plan.n_blocks
    size = n_blocks * width // n_row
    kept = plan.keep * plan.chunk_rows
    qb, n_sub, ratio, qs, rows = plan.view
    if plan.pitch > n_blocks:
        source = trail.reshape(*plan.view, n_blocks, width)
        buffer = pltpu.VMEM((2, n_sub, rows, plan.pitch, width), F32)
    else:
        source = trail.reshape(*plan.view[:4], rows * n_blocks, width)
        buffer = pltpu.VMEM((2, n_sub, rows * n_blocks, width), F32)

    def l_index(i, me, ids):
        b, h, s = plan.chunk_at(ids[plan.n_chunks + i])
        return (b, 0, h, s, 0, 0)

    whole = pl.BlockSpec(memory_space=pltpu.VMEM)
    resident = pltpu.VMEM((kept, n_blocks * width), BF16)
    n = plan.n_chunks * plan.chunk_rows
    out = pl.pallas_call(
        functools.partial(flip_body, plan, n_row),
        grid_spec=pltpu.PrefetchScalarGridSpec(
            num_scalar_prefetch=2,
            grid=(plan.n_chunks,),
            in_specs=[
                pl.BlockSpec(memory_space=pl.ANY),
                pl.BlockSpec((None, n_sub, None, None, rows, width), l_index),
            ],
            out_specs=[pl.BlockSpec((size, width), lambda i, me, ids: (0, 0))] * n_row + [whole, whole],
            scratch_shapes=[
                pltpu.VMEM((width, n_blocks * width), F32),
                pltpu.VMEM((n_blocks * width, width), F32),
                buffer,
                pltpu.SemaphoreType.DMA((2,)),
            ],
        ),
        out_shape=[jax.ShapeDtypeStruct((size, width), F32)] * n_row
        + [resident, resident],
        compiler_params=pltpu.CompilerParams(vmem_limit_bytes=FLIP_VMEM),
        cost_estimate=pl.CostEstimate(
            flops=6 * n * n_blocks * width * width, bytes_accessed=4 * n * n_blocks * width, transcendentals=0
        ),
        name="flip",
    )(me, ids, source, panel.reshape(*plan.view, width))
    return out[:n_row], out[n_row], out[n_row + 1]


def direct_body(n_blocks, group, half, ids_ref, s_ref, p_ref, *refs):
    away_ref, keep_ref, right = refs[-3:]
    step = pl.program_id(0)
    width = p_ref.shape[1]

    @pl.when(step == 0)
    def _():
        for g in range(n_blocks // group):
            high, low = split(p_ref[pl.ds(g * group * width, group * width), :])
            right[g, :, :width] = high
            right[g, :, width:] = low

    n_sub, sub_rows, _ = s_ref.shape
    rows = sub_rows // n_blocks

    def column(b):
        return jnp.concatenate([s_ref[i, pl.ds(b, rows, stride=n_blocks), :] for i in range(n_sub)], 0)

    both, rest = None, None
    for g in range(n_blocks // group):
        x = jnp.concatenate([column(g * group + b) for b in range(group)], 1)
        high, low = split(x)
        new_both = dot(high, right[g])
        new_rest = dot(low, right[g, :, :width])
        both = new_both if both is None else both + new_both
        rest = new_rest if rest is None else rest + new_rest
    result = both[:, :width] + both[:, width:] + rest

    @pl.when(step < half)
    def _():
        away_ref[...] = result

    @pl.when(step >= half)
    def _():
        keep_ref[...] = result


def direct_chunks(chunked, col_panel, ids, first, half, chunk_at, earlier=()):
    _, n_sub, _, _, sub_rows, width = chunked.shape
    n_blocks = col_panel.shape[0] // width
    group = math.gcd(n_blocks, 2)
    chunk_rows = n_sub * sub_rows // n_blocks

    def s_index(i, ids):
        qb, h, qs = chunk_at(ids[first + i])
        return (qb, 0, h, qs, 0, 0)

    out = jax.ShapeDtypeStruct((half * chunk_rows, width), F32)
    return pl.pallas_call(
        functools.partial(direct_body, n_blocks, group, half),
        grid_spec=pltpu.PrefetchScalarGridSpec(
            num_scalar_prefetch=1,
            grid=(2 * half,),
            in_specs=[
                pl.BlockSpec((None, n_sub, None, None, sub_rows, width), s_index),
                pl.BlockSpec((n_blocks * width, width), lambda i, ids: (0, 0)),
            ]
            + [pl.BlockSpec(memory_space=pl.ANY)] * len(earlier),
            out_specs=[
                pl.BlockSpec((chunk_rows, width), lambda i, ids: (jnp.minimum(i, half - 1), 0)),
                pl.BlockSpec((chunk_rows, width), lambda i, ids: (jnp.maximum(i - half, 0), 0)),
            ],
            scratch_shapes=[pltpu.VMEM((n_blocks // group, group * width, 2 * width), BF16)],
        ),
        out_shape=[out, out],
        compiler_params=pltpu.CompilerParams(vmem_limit_bytes=CHUNK_VMEM),
        cost_estimate=pl.CostEstimate(flops=1, bytes_accessed=1, transcendentals=0),
        name="direct",
    )(ids, chunked, col_panel, *earlier)


def kept_body(first, half, high_ref, low_ref, p_ref, *refs):
    away_ref, keep_ref, right = refs[-3:]
    step = pl.program_id(0)
    width = p_ref.shape[1]
    rows = away_ref.shape[0]

    @pl.when(step == 0)
    def _():
        high, low = split(p_ref[...])
        right[:, :width] = high
        right[:, width:] = low

    here = pl.ds(pl.multiple_of((first + step) * rows, rows), rows)
    both = dot(high_ref[here, :], right[...])
    result = both[:, :width] + both[:, width:] + dot(low_ref[here, :], right[:, :width])

    @pl.when(step < half)
    def _():
        away_ref[...] = result

    @pl.when(step >= half)
    def _():
        keep_ref[...] = result


def direct_kept(plan, high, low, col_panel, first, half, earlier=()):
    rows, width, depth = plan.chunk_rows, plan.width, col_panel.shape[0]
    out = jax.ShapeDtypeStruct((half * rows, width), F32)
    held = pl.BlockSpec(memory_space=pltpu.VMEM)
    return pl.pallas_call(
        functools.partial(kept_body, first, half),
        grid=(2 * half,),
        in_specs=[held, held, pl.BlockSpec((depth, width), lambda i: (0, 0))]
        + [pl.BlockSpec(memory_space=pl.ANY)] * len(earlier),
        out_specs=[
            pl.BlockSpec((rows, width), lambda i: (jnp.minimum(i, half - 1), 0)),
            pl.BlockSpec((rows, width), lambda i: (jnp.maximum(i - half, 0), 0)),
        ],
        out_shape=[out, out],
        scratch_shapes=[pltpu.VMEM((depth, 2 * width), BF16)],
        compiler_params=pltpu.CompilerParams(vmem_limit_bytes=DIRECT_VMEM),
        cost_estimate=pl.CostEstimate(flops=1, bytes_accessed=1, transcendentals=0),
        name="direct_kept",
    )(high, low, col_panel, *earlier)


def inverse_body(d_ref, o_ref):
    d = d_ref[...]
    width = d.shape[0]
    i = lax.broadcasted_iota(jnp.int32, d.shape, 0)
    j = lax.broadcasted_iota(jnp.int32, d.shape, 1)
    inv = jnp.where(i == j, 1.0 / d, 0.0)
    level = 0
    while (1 << level) < width:
        same = (i >> (level + 1)) == (j >> (level + 1))
        below = (i >> level) > (j >> level)
        part = jnp.where(jnp.logical_and(same, below), d, 0.0)
        inv = inv - full_dot(inv, full_dot(part, inv))
        level += 1
    o_ref[...] = inv


def inverse(diag_block):
    return pl.pallas_call(
        inverse_body,
        out_shape=jax.ShapeDtypeStruct(diag_block.shape, F32),
        compiler_params=pltpu.CompilerParams(vmem_limit_bytes=SMALL_VMEM),
        name="inverse",
    )(diag_block)


def over_rows(a, b, **kwargs):
    return lax.dot_general(a, b, (((0,), (0,)), ((), ())), preferred_element_type=F32, **kwargs)


def moment_body(n_parts, ids_ref, me_ref, *refs):
    parts, (p_ref, b_ref, l_ref, out_ref) = refs[:n_parts], refs[n_parts:]
    size, width = parts[0].shape
    product = jnp.zeros((width, width), F32)
    for k, part in enumerate(parts):
        start = pl.multiple_of((me_ref[0] ^ k) * size, size)
        p_high, p_low = split(p_ref[pl.ds(start, size), :])
        f_high, f_low = split(part[...])
        product += over_rows(p_high, f_high) + over_rows(p_high, f_low) + over_rows(p_low, f_high)
    b = b_ref[...].reshape(-1, width)
    l = l_ref[...].reshape(-1, width)
    out_ref[...] = over_rows(b, l, precision=HIGHEST) - product - product.T


def moment(plan, parts, col_panel, given, panel, ids, me):
    _, n_sub, _, _, rows = plan.view
    width = plan.width

    def at(i, ids, me):
        b, h, s = plan.chunk_at(ids[plan.mine])
        return (b, 0, h, s, 0, 0)

    def whole(shape):
        return pl.BlockSpec(shape, lambda i, ids, me: (0, 0))

    chunk = pl.BlockSpec((None, n_sub, None, None, rows, width), at)
    return pl.pallas_call(
        functools.partial(moment_body, len(parts)),
        grid_spec=pltpu.PrefetchScalarGridSpec(
            num_scalar_prefetch=2,
            grid=(1,),
            in_specs=[whole(x.shape) for x in parts] + [whole(col_panel.shape), chunk, chunk],
            out_specs=whole((width, width)),
        ),
        out_shape=jax.ShapeDtypeStruct((width, width), F32),
        compiler_params=pltpu.CompilerParams(vmem_limit_bytes=DIRECT_VMEM),
        name="moment",
    )(ids, me, *parts, col_panel, given.reshape(*plan.view, width), panel.reshape(*plan.view, width))


def gram_body(inv_ref, moment_ref, g_ref):
    g = -over_rows(inv_ref[...], moment_ref[...], precision=HIGHEST)
    i = lax.broadcasted_iota(jnp.int32, g.shape, 0)
    j = lax.broadcasted_iota(jnp.int32, g.shape, 1)
    g_ref[...] = jnp.where(i >= j, g, 0.0)


def gram_of(inv, total):
    return pl.pallas_call(
        gram_body,
        out_shape=jax.ShapeDtypeStruct(inv.shape, F32),
        compiler_params=pltpu.CompilerParams(vmem_limit_bytes=SMALL_VMEM),
        name="gram",
    )(inv, total)


def solve_body(n_terms, ids_ref, *refs):
    terms, inv_ref, b_ref, x_ref = refs[:n_terms], refs[n_terms], refs[-2], refs[-1]
    image = terms[0][...]
    for term in terms[1:]:
        image = image + term[...]
    total = b_ref[...].reshape(image.shape) - image
    x_ref[...] = full_dot(total, inv_ref[...])


def on_my_chunk(plan, body, ids, inputs, laid_out, out_shape, name):
    _, n_sub, _, _, rows = plan.view

    def at(i, ids):
        b, h, s = plan.chunk_at(ids[plan.mine])
        return (b, 0, h, s, 0, 0)

    def whole(shape):
        return pl.BlockSpec(shape, lambda i, ids: (0, 0))

    return pl.pallas_call(
        body,
        grid_spec=pltpu.PrefetchScalarGridSpec(
            num_scalar_prefetch=1,
            grid=(1,),
            in_specs=[whole(x.shape) for x in inputs]
            + [pl.BlockSpec((None, n_sub, None, None, rows, plan.width), at)],
            out_specs=whole(out_shape),
        ),
        out_shape=jax.ShapeDtypeStruct(out_shape, F32),
        compiler_params=pltpu.CompilerParams(vmem_limit_bytes=SMALL_VMEM),
        name=name,
    )(ids, *inputs, laid_out.reshape(*plan.view, plan.width))


def place_body(plan, slots, has_base, ids_ref, *refs):
    out_ref, sems = refs[-2:]
    pieces = refs[1:-2] if has_base else refs[:-2]
    _, n_sub, _, _, rows = plan.view
    copies = []
    for piece, (slot, half) in zip(pieces, slots):
        b, h, s = plan.chunk_at(ids_ref[slot])
        first, count = half * piece.shape[0], piece.shape[0]
        for i in range(n_sub):
            low, high = max(first, i * rows), min(first + count, (i + 1) * rows)
            if low < high:
                source = piece.at[pl.ds(low - first, high - low), :]
                target = out_ref.at[b, i, h, s, pl.ds(low - i * rows, high - low), :]
                copies.append(pltpu.make_async_copy(source, target, sems.at[len(copies)]))
    for copy in copies:
        copy.start()
    for copy in copies:
        copy.wait()


def place(plan, base, pieces, ids):
    anywhere = pl.BlockSpec(memory_space=pl.ANY)
    held = pl.BlockSpec(memory_space=pltpu.VMEM)
    bases = [] if base is None else [base]
    count = len(pieces) * (plan.view[1] + 1)
    return pl.pallas_call(
        functools.partial(place_body, plan, [piece[1:] for piece in pieces], base is not None),
        grid_spec=pltpu.PrefetchScalarGridSpec(
            num_scalar_prefetch=1,
            grid=(1,),
            in_specs=[anywhere] * len(bases) + [held] * len(pieces),
            out_specs=anywhere,
            scratch_shapes=[pltpu.SemaphoreType.DMA((count,))],
        ),
        out_shape=jax.ShapeDtypeStruct((*plan.view, plan.width), F32),
        input_output_aliases={1: 0} if bases else {},
        compiler_params=pltpu.CompilerParams(vmem_limit_bytes=SMALL_VMEM),
        name="place",
    )(ids, *bases, *[piece[0] for piece in pieces])


class Plan:
    def __init__(self, n_row, n_col, col_blocks, width):
        self.n_row, self.n_chunks = n_row, n_col
        self.n_blocks, self.width = col_blocks, width
        self.group = math.gcd(col_blocks, 2)
        qb = min(n_row, col_blocks)
        self.qs = n_row // qb
        self.view = (qb, col_blocks // qb, n_col // n_row, self.qs, width // self.qs)
        self.chunk_rows = self.view[1] * self.view[4]
        self.pitch = col_blocks
        if col_blocks % 16 == 0:
            self.pitch = col_blocks + 8
        n_z = n_col // 2
        self.far = n_z // 2
        self.steps, self.offsets, self.twins = [], [], []
        for distance in range(self.far, -1, -1):
            here = sorted({distance % n_z, -distance % n_z})
            self.steps.append((len(self.offsets), here))
            self.offsets += here + here
            if distance == 0:
                self.mine = len(self.offsets) - 1
            self.twins += [1] * len(here) + [0] * len(here)
        fits = KEEP_BYTES // (4 * self.chunk_rows * col_blocks * width)
        self.slots, held = {}, []
        for begin, here in sorted(self.steps, key=lambda step: step[1][0] == 0):
            places = range(begin, begin + 2 * len(here))
            if len(held) + len(places) <= fits:
                self.slots[begin] = len(held)
                held += places
        self.keep = len(held)
        self.skip = self.n_chunks - self.keep
        self.flip_order = [p for p in range(self.n_chunks) if p not in held] + held

    def chunk_at(self, chunk):
        h, q = chunk // self.n_row, chunk % self.n_row
        return q // self.qs, h, q % self.qs


def per_device(trail_adjoint, panel, panel_adjoint, diag_block):
    width = diag_block.shape[0]
    n_row = lax.axis_size("row")
    n_col = lax.axis_size("col")
    ratio = n_col // n_row
    n_z = n_col // 2
    row_blocks = panel.shape[0]
    col_blocks = trail_adjoint.shape[2]
    plan = Plan(n_row, n_col, col_blocks, width)
    row_index = lax.axis_index("row")
    col_index = lax.axis_index("col")
    z, core = col_index // 2, col_index % 2
    move = functools.partial(send, n_row=n_row, n_col=n_col)
    up = lambda r, c: (r, (c + 2) % n_col)
    down = lambda r, c: (r, (c - 2) % n_col)
    twin = lambda r, c: (r, c ^ 1)
    places = list(range(plan.n_chunks)) + plan.flip_order
    offsets = jnp.array([plan.offsets[p] for p in places], jnp.int32)
    twins = jnp.array([plan.twins[p] for p in places], jnp.int32)
    ids = (z + offsets) % n_z * 2 + (core ^ twins)

    def to_panel_user(r, c):
        h, s = divmod(c, n_row)
        return r ^ (((r ^ s) + 1) % n_row), h * n_row + r

    chosen = choose(panel.reshape(col_blocks, ratio, width, width), (col_index // n_row).reshape(1))
    col_panel = move(chosen.reshape(col_blocks * width, width), to_panel_user)

    me = row_index.reshape(1)
    parts, high, low = flip_parts(plan, trail_adjoint, panel, ids, me, n_row)
    arrived = [move(parts[k], lambda r, c: (r ^ k, c)) for k in range(1, n_row)]
    flip_sum = sum(arrived, parts[0])
    flipped = move(flip_sum, lambda r, c: (c % n_row, c // n_row * n_row + r))
    inv = inverse(diag_block)

    moments = [moment(plan, parts, col_panel, panel_adjoint, panel, ids, me)]
    bit = 1
    while bit < n_row:
        moments.append(moments[-1] + move(moments[-1], lambda r, c: (r ^ bit, c)))
        bit *= 2
    row_steps = len(moments) - 1

    def later(*arrays, times=1):
        few = sum(x[:8] for x in arrays)
        for _ in range(times):
            few = move(few, twin)
        return few

    rows = plan.chunk_rows
    cut = rows // 2
    sent = []
    for begin, here in plan.steps:
        if here[0] == 0:
            earlier = totals
        elif begin:
            earlier = totals + [flip_sum, moments[1]]
        else:
            earlier = [inv]
        right = col_panel
        if begin in plan.slots:
            away, keep = direct_kept(plan, high, low, right, plan.slots[begin], len(here), earlier)
        else:
            chunked = trail_adjoint.reshape(*plan.view[:4], plan.view[4] * col_blocks, width)
            away, keep = direct_chunks(chunked, right, ids, begin, len(here), plan.chunk_at, earlier)
        totals = []
        for k in range(len(here)):
            piece = slice(k * rows, (k + 1) * rows)
            totals.append(keep[piece] + move(away[piece], twin))
        if here[0] == 0:
            own = totals[0]
        else:
            sent += [
                move(total, lambda r, c: (r, (c + 2 * distance) % n_col)) for distance, total in zip(here, totals)
            ]
    mine = [own, flipped] + sent

    bit = 1
    while bit < n_z:
        moments.append(moments[-1] + move(moments[-1], lambda r, c: (r, c ^ (2 * bit))))
        bit *= 2
    x = on_my_chunk(
        plan, functools.partial(solve_body, len(mine)), ids, mine + [inv] + [later(*sent)], panel_adjoint, (rows, width), "solve"
    )

    lower, upper = {0: x[:cut]}, {0: x[cut:]}
    below, above = (x[:cut], x[cut:]), (x[cut:], x[:cut])
    for distance in range(1, plan.far):
        below, above = [move(b, up) for b in below], [move(a, down) for a in above]
        lower[-distance % n_z], upper[-distance % n_z] = below
        upper[distance], lower[distance] = above
    go_up, go_down = below[0], above[0]
    lower[plan.far], upper[plan.far] = move(go_up, up), move(go_down, down)
    order = (z + jnp.arange(n_z, dtype=jnp.int32)) % n_z * 2
    place_ids = jnp.concatenate([order + core, order + (1 - core)])
    near = [d for d in range(n_z) if d != plan.far]
    pieces = [(lower[d], d, 0) for d in near] + [(upper[d], d, 1) for d in near]
    pieces += [(move(piece, twin), n_z + d, half) for piece, d, half in pieces]
    solved = place(plan, None, pieces, place_ids)
    gram = gram_of(inv, moments[-1] + move(moments[-1], twin))
    (lower[plan.far], upper[plan.far]), (solved, gram) = lax.optimization_barrier(
        ((lower[plan.far], upper[plan.far]), (solved, gram))
    )
    last = [(lower[plan.far], plan.far, 0), (upper[plan.far], plan.far, 1)]
    last += [(move(piece, twin), n_z + d, half) for piece, d, half in last]
    solved = place(plan, solved, last, place_ids)
    return solved.reshape(row_blocks, width, width), gram


def solution(mesh):
    in_specs = (P(None, "row", None, "col"), P(None, "row", None), P(None, "row", None), P())
    out_specs = (P(None, "row", None), P())
    return jax.shard_map(
        per_device, mesh=mesh, in_specs=in_specs, out_specs=out_specs, check_vma=False
    )
```
